512 devices in a mesh: wide: 64 (over y, x, z_lo), narrow: 8 (over z_hi, core).
Axes of the slice: x: 4, y: 8, z: 8 (z_hi: 4, z_lo: 2; z = z_hi * 2 + z_lo), core: 2. Of those that a mesh axis runs over, the one named last changes fastest.
Arguments:
- tval: bfloat16 [4096, 12, 128, 128], P(('wide', 'narrow')), may hold values from -0.16992188 to 0.16992188
- tcol: int32 [4096, 12], replicated, may hold values from 0 to 4095, as said below
- ocol: int32 [4096, 12], P(('wide', 'narrow')), may hold values from 0 to 4095, as said below
- basis: bfloat16 [524288, 128], P(('wide', 'narrow')), may hold values from -6 to 6
Outputs:
- projected: bfloat16 [524288, 128], P(('wide', 'narrow'))
- level: float32 [128, 128], replicated
The draws below stay inside these ranges and needn't reach their ends.
Inputs may be any that keep to these rules, and one draw needn't show every extreme that they name: `tcol`: the 12 block columns of row i are distinct, include i, and each lies within cyclic distance 8 of i modulo 4096. `ocol`: the 12 block columns of row i are distinct, include i, and each lies within cyclic distance 8 of i modulo 4096.
All inputs are finite; a program needn't handle non-finite values.
Results may differ from the reference program's by a relative error of at most 0.0049.
Values may be sent and summed in bfloat16 or wider, within the bound.
No kernel may reach another device: no remote copies, remote signals or barrier semaphores. Data moves between devices by JAX's collectives and lax.ppermute only.
A program may use at most 64 MiB of HBM per device.

```python
import jax
import jax.numpy as jnp
from jax import lax

B = 128
SLOTS = 12
K = 128
BAND = 8
NBR = 4096


def banded_pattern(key):
    keys = jax.random.split(key, NBR)
    offsets = jnp.concatenate([jnp.arange(-BAND, 0, dtype=jnp.int32), jnp.arange(1, BAND + 1, dtype=jnp.int32)])
    picks = jax.vmap(lambda k: jax.random.permutation(k, offsets))(keys)[:, :SLOTS - 1]
    shifts = jnp.concatenate([jnp.zeros((NBR, 1), jnp.int32), picks], axis=1)
    return (jnp.arange(NBR, dtype=jnp.int32)[:, None] + shifts) % NBR


def draw_tcol(key, part):
    key = jax.random.fold_in(key, 11)
    return banded_pattern(key)


def draw_ocol(key, part):
    key = jax.random.fold_in(key, 23)
    return banded_pattern(key)


def block_scale(key, dims, shards, least, largest):
    def one(position, shards_of):
        steps = jax.random.uniform(jax.random.fold_in(jax.random.fold_in(key, 6), position), (shards_of,), jnp.float32, least / len(shards), largest / len(shards))
        return jnp.repeat(jnp.exp(steps), dims[position] // shards_of).reshape((-1,) + (1,) * (len(dims) - position - 1))

    loudness = one(*shards[0])
    for cut in shards[1:]:
        loudness = loudness * one(*cut)
    return loudness


def gaussian(key, extent, scale, bound, pieces=(), held_as=jnp.bfloat16):
    drawn = scale * jax.random.normal(key, extent, jnp.float32)
    if pieces:
        drawn = drawn * block_scale(key, extent, pieces, -0.22, 0.18)
    return jnp.clip(drawn, -bound, bound).astype(held_as)


def setup_inputs(seed: int = 0) -> dict:
    key_of = jax.random.split(jax.random.key(seed), 5)
    tval = gaussian(key_of[0], (NBR, SLOTS, B, B), 0.028, 0.16992188, ((0, 512),))
    tcol = draw_tcol(jax.random.fold_in(key_of[4], 71), 0)
    ocol = draw_ocol(jax.random.fold_in(key_of[4], 71), 0)
    basis = gaussian(key_of[3], (NBR * B, K), 1.0, 6.0, ((0, 512),))
    return {"tval": tval, "tcol": tcol, "ocol": ocol, "basis": basis}


def reference(tval, tcol, ocol, basis):
    count = tval.shape[0]
    size = tval.shape[2]
    width = basis.shape[1]
    basis_blocks = basis.reshape(count, size, width)

    def one_row(index):
        cols = tcol[index]
        lhs = tval[index].astype(jnp.float32)
        rows = tval[cols].astype(jnp.float32)
        pattern = tcol[cols]
        outcols = ocol[index]
        match = (pattern[None, :, :] == outcols[:, None, None]).astype(jnp.float32)
        selected = jnp.einsum('ost,stbc->sobc', match, rows, precision=lax.Precision.HIGHEST)
        square = jnp.einsum('sab,sobc->oac', lhs, selected, precision=lax.Precision.HIGHEST).astype(jnp.bfloat16)
        picked = basis_blocks[outcols].astype(jnp.float32)
        result = jnp.einsum('oac,ock->ak', square.astype(jnp.float32), picked, precision=lax.Precision.HIGHEST)
        return result.astype(jnp.bfloat16)
    projected = lax.map(one_row, jnp.arange(count, dtype=jnp.int32)).reshape(count * size, width)
    level = jnp.dot(basis.T, projected, preferred_element_type=jnp.float32)
    level = level / jnp.sqrt(jnp.float32(count * size))
    return (projected, level)
```

```python
import jax
import jax.numpy as jnp
from jax import lax
from jax.experimental import pallas as pl
from jax.experimental.pallas import tpu as pltpu
from jax.sharding import Mesh
from jax.sharding import PartitionSpec as P

LOCAL = 8
B = 128
SLOTS = 12
PAIRS = 36
RANKS = ("y", "x", "zl", "zh", "core")
RING = ("zl", "zh", "core")
PLANE = ("y", "x")


def right_place(r, j):
    return r * (r + 1) // 2 + j


def left_place(r, j):
    return LOCAL * r - r * (r - 1) // 2 + j - r


def pack_kernel(tcol, tval, to_right, to_left, table, sems):
    for p in range(2 * PAIRS):
        table[p] = 0
    for r in range(LOCAL):
        for s in range(SLOTS):
            v = tcol[LOCAL + r, s]
            place = jnp.where(
                v >= 2 * LOCAL,
                r * (r + 1) // 2 + v - 2 * LOCAL,
                jnp.where(v < LOCAL, PAIRS + LOCAL * r - r * (r - 1) // 2 + v - r, 2 * PAIRS),
            )
            table[place] = s
    copies = []
    for r in range(LOCAL):
        for j in range(LOCAL):
            if j <= r:
                p = right_place(r, j)
                copies.append(
                    pltpu.make_async_copy(tval.at[r, table[p]], to_right.at[:, pl.ds(p * B, B)], sems.at[p])
                )
                copies[-1].start()
            if j >= r:
                p = left_place(r, j)
                copies.append(
                    pltpu.make_async_copy(
                        tval.at[r, table[PAIRS + p]], to_left.at[:, pl.ds(p * B, B)], sems.at[PAIRS + p]
                    )
                )
                copies[-1].start()
    for copy in copies:
        copy.wait()


def pack(tcol, tval):
    out = jax.ShapeDtypeStruct((B, PAIRS * B), jnp.bfloat16)
    return pl.pallas_call(
        pack_kernel,
        out_shape=(out, out),
        in_specs=[pl.BlockSpec(memory_space=pltpu.SMEM), pl.BlockSpec(memory_space=pl.ANY)],
        out_specs=(pl.BlockSpec(memory_space=pl.ANY), pl.BlockSpec(memory_space=pl.ANY)),
        scratch_shapes=[pltpu.SMEM((2 * PAIRS + 1,), jnp.int32), pltpu.SemaphoreType.DMA((2 * PAIRS,))],
        name="pack",
    )(tcol, tval)


def inner_kernel(tcol, wanted, held, tval, basis_l, basis, basis_r, y_out, p_out, level, basis_t, blocks, z, y_own):
    for part, ref in enumerate((basis_l, basis, basis_r)):
        blocks[part * LOCAL * B : (part + 1) * LOCAL * B, :] = ref[: LOCAL * B, :]
    y_own[LOCAL * LOCAL * B :, :] = jnp.zeros((B, B), jnp.bfloat16)

    @pl.loop(0, LOCAL)
    def _(j):
        for s in range(SLOTS):
            c = tcol[LOCAL + j, s]
            z[s] = jnp.dot(
                tval[j, s],
                blocks[pl.ds(pl.multiple_of(c * B, B), B), :],
                preferred_element_type=jnp.float32,
            )

        @pl.loop(0, 2 * LOCAL + 1)
        def _(d):
            i = j + d
            r = i & (LOCAL - 1)
            part = i >> 3
            own = part == 1
            place = jnp.where(part == 0, (r * (r + 1) >> 1) + j, PAIRS + LOCAL * r - (r * (r - 1) >> 1) + j - r)
            place = jnp.where(own, r * LOCAL + j, place)
            rows = pl.ds(pl.multiple_of(place * B, B), B)
            on = held[i, j]

            def total():
                y = jnp.zeros((B, B), jnp.float32)
                for s in range(SLOTS):
                    y = y + wanted[i, tcol[LOCAL + j, s]] * z[s]
                return y.astype(jnp.bfloat16)

            @pl.when(jnp.logical_and(own, on == 1))
            def _():
                y_own[rows, :] = total()

            @pl.when(jnp.logical_and(jnp.logical_not(own), on == 1))
            def _():
                y_out[rows, :] = total()

            @pl.when(jnp.logical_and(jnp.logical_not(own), on == 0))
            def _():
                y_out[rows, :] = jnp.zeros((B, B), jnp.bfloat16)

    level[...] = jnp.zeros((B, B), jnp.float32)

    @pl.loop(0, LOCAL)
    def _(r):
        p = jnp.zeros((B, B), jnp.float32)
        for s in range(SLOTS):
            v = tcol[LOCAL + r, s] - LOCAL
            inside = jnp.logical_and(v >= 0, v < LOCAL)
            place = jnp.where(inside, r * LOCAL + v, LOCAL * LOCAL)
            p = p + jnp.dot(
                tval[r, s],
                y_own[pl.ds(pl.multiple_of(place * B, B), B), :],
                preferred_element_type=jnp.float32,
            )
        rows = pl.ds(pl.multiple_of(r * B, B), B)
        p_out[rows, :] = p
        level[...] += lax.dot_general(
            basis[rows, :], p.astype(jnp.bfloat16), (((0,), (0,)), ((), ())), preferred_element_type=jnp.float32
        )

    for part, ref in enumerate((basis_l, basis_r)):
        for r in range(LOCAL):
            place = (part * LOCAL + r) * B
            basis_t[:, place : place + B] = ref[r * B : (r + 1) * B, :].T


def inner(tcol, wanted, held, tval, basis_l, basis, basis_r):
    vmem = pl.BlockSpec(memory_space=pltpu.VMEM)
    smem = pl.BlockSpec(memory_space=pltpu.SMEM)
    return pl.pallas_call(
        inner_kernel,
        out_shape=(
            jax.ShapeDtypeStruct((2 * PAIRS * B, B), jnp.bfloat16),
            jax.ShapeDtypeStruct((LOCAL * B, B), jnp.float32),
            jax.ShapeDtypeStruct((B, B), jnp.float32),
            jax.ShapeDtypeStruct((B, 2 * LOCAL * B), jnp.bfloat16),
        ),
        in_specs=[smem, smem, smem, vmem, vmem, vmem, vmem],
        out_specs=(vmem, vmem, vmem, vmem),
        scratch_shapes=[
            pltpu.VMEM((3 * LOCAL * B, B), jnp.bfloat16),
            pltpu.VMEM((SLOTS, B, B), jnp.float32),
            pltpu.VMEM(((LOCAL * LOCAL + 1) * B, B), jnp.bfloat16),
        ],
        compiler_params=pltpu.CompilerParams(vmem_limit_bytes=28 * 1024 * 1024),
        cost_estimate=pl.CostEstimate(flops=12_000_000_000, bytes_accessed=8_000_000, transcendentals=0),
        name="inner",
    )(tcol, wanted, held, tval, basis_l, basis, basis_r)


def outer_kernel(from_left, from_right, y, basis_t, level_in, p_left, p_right, level):
    total = level_in[...]
    for r in range(LOCAL):
        at = right_place(r, 0) * B
        span = (r + 1) * B
        p = jnp.dot(from_left[:, at : at + span], y[at : at + span, :], preferred_element_type=jnp.float32)
        p_left[r * B : (r + 1) * B, :] = p.astype(jnp.bfloat16)
    for r in range(LOCAL):
        at = left_place(r, r) * B
        span = (LOCAL - r) * B
        p = jnp.dot(
            from_right[:, at : at + span],
            y[PAIRS * B + at : PAIRS * B + at + span, :],
            preferred_element_type=jnp.float32,
        )
        p_right[r * B : (r + 1) * B, :] = p.astype(jnp.bfloat16)
    total += jnp.dot(basis_t[:, : LOCAL * B], p_left[...], preferred_element_type=jnp.float32)
    total += jnp.dot(basis_t[:, LOCAL * B :], p_right[...], preferred_element_type=jnp.float32)
    level[...] = total


def outer(from_left, from_right, y, basis_t, level):
    vmem = pl.BlockSpec(memory_space=pltpu.VMEM)
    rows = jax.ShapeDtypeStruct((LOCAL * B, B), jnp.bfloat16)
    return pl.pallas_call(
        outer_kernel,
        out_shape=(rows, rows, jax.ShapeDtypeStruct((B, B), jnp.float32)),
        in_specs=[vmem] * 5,
        out_specs=(vmem, vmem, vmem),
        compiler_params=pltpu.CompilerParams(vmem_limit_bytes=20 * 1024 * 1024),
        name="outer",
    )(from_left, from_right, y, basis_t, level)


def copies(part, count):
    return jnp.broadcast_to(part[None], (count,) + part.shape)


def per_device(tval, tcol, ocol, basis):
    devices = lax.axis_size(RANKS)
    count = LOCAL * devices
    me = lax.axis_index(RANKS)
    first = me * LOCAL
    onward = [(i, (i + 1) % devices) for i in range(devices)]
    back = [((i + 1) % devices, i) for i in range(devices)]

    ring = lax.axis_size(RING)
    plane = lax.axis_size(PLANE)

    places = (ocol - first + 2 * LOCAL + count) % count
    mine = jnp.any(places[:, :, None] == jnp.arange(B, dtype=jnp.int32), axis=1).astype(jnp.bfloat16)
    sent = jnp.concatenate([basis, mine, jnp.zeros_like(mine)], axis=0)
    basis_l = lax.ppermute(sent, RANKS, onward)
    basis_r = lax.ppermute(sent, RANKS, back)

    near = jnp.concatenate(
        [lax.dynamic_slice_in_dim(tcol, ((me + k) % devices) * LOCAL, LOCAL, 0) for k in (devices - 1, 0, 1)]
    )
    near = (near - first + LOCAL + count) % count
    held = jnp.any(near[:, :, None] == LOCAL + jnp.arange(LOCAL, dtype=jnp.int32), axis=1).astype(jnp.int32)
    to_right, to_left = pack(near, tval)
    from_left = lax.ppermute(to_right, RANKS, onward)
    from_right = lax.ppermute(to_left, RANKS, back)

    rows = LOCAL * B
    wanted = jnp.concatenate(
        [
            basis_l[rows : rows + LOCAL, 2 * LOCAL : 5 * LOCAL],
            mine[:, LOCAL : 4 * LOCAL],
            basis_r[rows : rows + LOCAL, : 3 * LOCAL],
        ]
    ).astype(jnp.float32)
    y, p_own, level, basis_t = inner(near, wanted, held, tval, basis_l, basis, basis_r)
    p_left, p_right, level = outer(from_left, from_right, y, basis_t, level)

    theirs_r = lax.ppermute(p_left, RANKS, back)
    theirs_l = lax.ppermute(p_right, RANKS, onward)

    level = lax.all_to_all(level.reshape(ring, B // ring, B), RING, 0, 0).sum(0)
    level = lax.all_to_all(copies(level, plane), PLANE, 0, 0).sum(0)
    level = level / jnp.sqrt(jnp.float32(count * B))
    level = lax.all_to_all(copies(level, ring), RING, 0, 0).reshape(B, B)

    projected = p_own + theirs_l.astype(jnp.float32) + theirs_r.astype(jnp.float32)
    return (projected.astype(jnp.bfloat16), level)


def solution(mesh):
    mesh = Mesh(mesh.devices.reshape(8, 4, 2, 4, 2), RANKS)
    return jax.shard_map(
        per_device,
        mesh=mesh,
        in_specs=(P(RANKS, None, None, None), P(), P(RANKS, None), P(RANKS, None)),
        out_specs=(P(RANKS, None), P()),
        check_vma=False,
    )
```

```python
import functools

import jax
import jax.numpy as jnp
from jax import lax
from jax.experimental import pallas as pl
from jax.experimental.pallas import tpu as pltpu
from jax.sharding import Mesh
from jax.sharding import PartitionSpec as P

LOCAL = 8
B = 128
SLOTS = 12
PAIRS = 36
RANKS = ("y", "x", "zl", "zh", "core")
RING = ("zl", "zh", "core")
PLANE = ("y", "x")


def pair_place(a, b):
    return a * (a + 1) // 2 + b


def is_odd():
    return lax.axis_index("core") == 1


def mark_kernel(count, ocol, basis, sent, sem):
    fetch = pltpu.make_async_copy(basis, sent.at[pl.ds(0, LOCAL * B), :], sem)
    fetch.start()
    first = lax.axis_index(RANKS) * LOCAL
    row = lax.broadcasted_iota(jnp.int32, (2 * LOCAL, B), 0)
    lane = lax.broadcasted_iota(jnp.int32, (2 * LOCAL, B), 1)
    marks = jnp.zeros((2 * LOCAL, B), jnp.float32)
    for r in range(LOCAL):
        mark = lane < 0
        for s in range(SLOTS):
            mark = jnp.logical_or(mark, lane == lax.rem(ocol[r, s] - first + 2 * LOCAL + count, count))
        marks = jnp.where(jnp.logical_and(mark, row == r), 1.0, marks)
    sent[LOCAL * B :, :] = marks.astype(jnp.bfloat16)
    fetch.wait()


def mark(count, ocol, basis):
    return pl.pallas_call(
        functools.partial(mark_kernel, count),
        out_shape=jax.ShapeDtypeStruct((LOCAL * B + 2 * LOCAL, B), jnp.bfloat16),
        in_specs=[pl.BlockSpec(memory_space=pltpu.SMEM), pl.BlockSpec(memory_space=pl.ANY)],
        out_specs=pl.BlockSpec(memory_space=pltpu.VMEM),
        scratch_shapes=[pltpu.SemaphoreType.DMA],
        compiler_params=pltpu.CompilerParams(vmem_limit_bytes=56 * 1024 * 1024),
        name="mark",
    )(ocol, basis)


def pack_kernel(count, tcol, tval_hbm, to_far, to_near, table, tval, sem):
    fetch = pltpu.make_async_copy(tval_hbm, tval, sem)
    fetch.start()
    odd = is_odd()
    first = lax.axis_index(RANKS) * LOCAL
    far_right = jnp.where(odd, 0, PAIRS)
    far_left = PAIRS - far_right
    for p in range(2 * PAIRS):
        table[p] = 0
    for r in range(LOCAL):
        for s in range(SLOTS):
            v = lax.rem(tcol[r, s] - first + LOCAL + count, count)
            place = jnp.where(
                v >= 2 * LOCAL,
                far_right + pair_place(r, 0) + v - 2 * LOCAL,
                jnp.where(v < LOCAL, far_left + pair_place(LOCAL - 1 - r, 0) + LOCAL - 1 - v, 2 * PAIRS),
            )
            table[place] = s
    fetch.wait()
    for a in range(LOCAL):
        far_row = jnp.where(odd, a, LOCAL - 1 - a)
        near_row = LOCAL - 1 - far_row
        for b in range(a + 1):
            p = pair_place(a, b)
            to_far[:, p * B : (p + 1) * B] = tval[far_row, table[p]]
            to_near[:, p * B : (p + 1) * B] = tval[near_row, table[PAIRS + p]]


def pack(count, tcol, tval):
    out = jax.ShapeDtypeStruct((B, PAIRS * B), jnp.bfloat16)
    vmem = pl.BlockSpec(memory_space=pltpu.VMEM)
    return pl.pallas_call(
        functools.partial(pack_kernel, count),
        out_shape=(out, out),
        in_specs=[pl.BlockSpec(memory_space=pltpu.SMEM), pl.BlockSpec(memory_space=pl.ANY)],
        out_specs=(vmem, vmem),
        scratch_shapes=[
            pltpu.SMEM((2 * PAIRS + 1,), jnp.int32),
            pltpu.VMEM((LOCAL, SLOTS, B, B), jnp.bfloat16),
            pltpu.SemaphoreType.DMA,
        ],
        compiler_params=pltpu.CompilerParams(vmem_limit_bytes=56 * 1024 * 1024),
        name="pack",
    )(tcol, tval)


def inner_kernel(tcol, wanted, held, tval, basis_far, basis, basis_near, y_out, p_out, level, basis_t, blocks, z, y_own, t_own, table):
    odd = is_odd()
    size = LOCAL * B
    far_at = jnp.where(odd, 2 * size, 0)
    blocks[pl.ds(pl.multiple_of(far_at, size), size), :] = basis_far[:size, :]
    blocks[size : 2 * size, :] = basis[...]
    blocks[pl.ds(pl.multiple_of(2 * size - far_at, size), size), :] = basis_near[:size, :]
    for p in range(LOCAL * LOCAL):
        table[p] = 0
    for r in range(LOCAL):
        for s in range(SLOTS):
            v = tcol[LOCAL + r, s] - LOCAL
            inside = jnp.logical_and(v >= 0, v < LOCAL)
            table[jnp.where(inside, r * LOCAL + v, LOCAL * LOCAL)] = s

    @pl.loop(0, LOCAL)
    def _(j):
        for s in range(SLOTS):
            c = tcol[LOCAL + j, s]
            z[s] = jnp.dot(
                tval[j, s],
                blocks[pl.ds(pl.multiple_of(c * B, B), B), :],
                preferred_element_type=jnp.float32,
            )

        @pl.loop(0, 2 * LOCAL + 1)
        def _(d):
            i = j + d
            r = i & (LOCAL - 1)
            part = i >> 3
            own = part == 1
            left = part == 0
            a = jnp.where(left, r, LOCAL - 1 - r)
            b = jnp.where(left, j, LOCAL - 1 - j)
            place = (a * (a + 1) >> 1) + b + jnp.where(left == odd, PAIRS, 0)
            place = jnp.where(own, r * LOCAL + j, place)
            rows = pl.ds(pl.multiple_of(place * B, B), B)
            on = held[i, j]

            def total():
                y = jnp.zeros((B, B), jnp.float32)
                for s in range(SLOTS):
                    y = y + wanted[i, tcol[LOCAL + j, s]] * z[s]
                return y.astype(jnp.bfloat16)

            @pl.when(jnp.logical_and(own, on == 1))
            def _():
                y_own[rows, :] = total()

            @pl.when(jnp.logical_and(jnp.logical_not(own), on == 1))
            def _():
                y_out[rows, :] = total()

            @pl.when(jnp.logical_and(own, on == 0))
            def _():
                y_own[rows, :] = jnp.zeros((B, B), jnp.bfloat16)

            @pl.when(jnp.logical_and(jnp.logical_not(own), on == 0))
            def _():
                y_out[rows, :] = jnp.zeros((B, B), jnp.bfloat16)

    level[...] = jnp.zeros((B, B), jnp.float32)

    for r in range(LOCAL):
        for j in range(LOCAL):
            t_own[r % 2, :, j * B : (j + 1) * B] = tval[r, table[r * LOCAL + j]]
        size = LOCAL * B
        p = jnp.dot(
            t_own[r % 2], y_own[r * size : (r + 1) * size, :], preferred_element_type=jnp.float32
        )
        rows = slice(r * B, (r + 1) * B)
        p_out[rows, :] = p
        level[...] += lax.dot_general(
            basis[rows, :], p.astype(jnp.bfloat16), (((0,), (0,)), ((), ())), preferred_element_type=jnp.float32
        )

    for part, ref in enumerate((basis_far, basis_near)):
        for r in range(LOCAL):
            place = (part * LOCAL + r) * B
            basis_t[:, place : place + B] = ref[r * B : (r + 1) * B, :].T


def inner(tcol, wanted, held, tval, basis_far, basis, basis_near):
    vmem = pl.BlockSpec(memory_space=pltpu.VMEM)
    smem = pl.BlockSpec(memory_space=pltpu.SMEM)
    return pl.pallas_call(
        inner_kernel,
        out_shape=(
            jax.ShapeDtypeStruct((2 * PAIRS * B, B), jnp.bfloat16),
            jax.ShapeDtypeStruct((LOCAL * B, B), jnp.float32),
            jax.ShapeDtypeStruct((B, B), jnp.float32),
            jax.ShapeDtypeStruct((B, 2 * LOCAL * B), jnp.bfloat16),
        ),
        in_specs=[smem, smem, smem, vmem, vmem, vmem, vmem],
        out_specs=(vmem, vmem, vmem, vmem),
        scratch_shapes=[
            pltpu.VMEM((3 * LOCAL * B, B), jnp.bfloat16),
            pltpu.VMEM((SLOTS, B, B), jnp.float32),
            pltpu.VMEM((LOCAL * LOCAL * B, B), jnp.bfloat16),
            pltpu.VMEM((2, B, LOCAL * B), jnp.bfloat16),
            pltpu.SMEM((LOCAL * LOCAL + 1,), jnp.int32),
        ],
        compiler_params=pltpu.CompilerParams(vmem_limit_bytes=28 * 1024 * 1024),
        cost_estimate=pl.CostEstimate(flops=12_000_000_000, bytes_accessed=8_000_000, transcendentals=0),
        name="inner",
    )(tcol, wanted, held, tval, basis_far, basis, basis_near)


def outer_kernel(side, received, y, basis_t, level_in, p_out, level):
    odd = is_odd()
    for a in range(LOCAL):
        at = pair_place(a, 0) * B
        span = (a + 1) * B
        row = jnp.where(odd == (side == 0), LOCAL - 1 - a, a)
        p = jnp.dot(received[:, at : at + span], y[at : at + span, :], preferred_element_type=jnp.float32)
        p_out[pl.ds(pl.multiple_of(row * B, B), B), :] = p.astype(jnp.bfloat16)
    level[...] = level_in[...] + jnp.dot(basis_t[...], p_out[...], preferred_element_type=jnp.float32)


def outer(side, received, y, basis_t, level, name):
    vmem = pl.BlockSpec(memory_space=pltpu.VMEM)
    rows = LOCAL * B
    return pl.pallas_call(
        functools.partial(outer_kernel, side),
        grid=(1,),
        out_shape=(jax.ShapeDtypeStruct((rows, B), jnp.bfloat16), jax.ShapeDtypeStruct((B, B), jnp.float32)),
        in_specs=[
            vmem,
            pl.BlockSpec((PAIRS * B, B), lambda i: (side, 0)),
            pl.BlockSpec((B, rows), lambda i: (0, side)),
            vmem,
        ],
        out_specs=(vmem, vmem),
        compiler_params=pltpu.CompilerParams(vmem_limit_bytes=20 * 1024 * 1024),
        cost_estimate=pl.CostEstimate(flops=400_000_000, bytes_accessed=3_000_000, transcendentals=0),
        name=name,
    )(received, y, basis_t, level)


def copies(part, count):
    return jnp.broadcast_to(part[None], (count,) + part.shape)


def per_device(tval, tcol, ocol, basis):
    devices = lax.axis_size(RANKS)
    count = LOCAL * devices
    me = lax.axis_index(RANKS)
    first = me * LOCAL
    near = [(i, i ^ 1) for i in range(devices)]
    far = [(i, (i + 1) % devices if i % 2 else (i - 1) % devices) for i in range(devices)]
    ring = lax.axis_size(RING)
    plane = lax.axis_size(PLANE)

    cols = jnp.concatenate(
        [lax.dynamic_slice_in_dim(tcol, ((me + k) % devices) * LOCAL, LOCAL, 0) for k in (devices - 1, 0, 1)]
    )
    cols = (cols - first + LOCAL + count) % count
    sent = mark(count, ocol, basis)
    basis_far = lax.ppermute(sent, RANKS, far)
    basis_near = lax.ppermute(sent, RANKS, near)
    to_far, to_near = pack(count, lax.dynamic_slice_in_dim(tcol, first, LOCAL, 0), tval)
    from_far = lax.ppermute(to_far, RANKS, far)
    from_near = lax.ppermute(to_near, RANKS, near)

    held = jnp.any(cols[:, :, None] == LOCAL + jnp.arange(LOCAL, dtype=jnp.int32), axis=1).astype(jnp.int32)
    rows = LOCAL * B
    odd = is_odd()
    far_marks, near_marks = (part[rows : rows + LOCAL] for part in (basis_far, basis_near))
    wanted = jnp.concatenate(
        [
            jnp.where(odd, near_marks, far_marks)[:, 2 * LOCAL : 5 * LOCAL],
            sent[rows : rows + LOCAL, LOCAL : 4 * LOCAL],
            jnp.where(odd, far_marks, near_marks)[:, : 3 * LOCAL],
        ]
    ).astype(jnp.float32)
    y, p_own, level, basis_t = inner(cols, wanted, held, tval, basis_far, basis, basis_near)
    p_near, level = outer(1, from_near, y, basis_t, level, "outer_near")
    p_far, level = outer(0, from_far, y, basis_t, level, "outer_far")

    theirs_far = lax.ppermute(p_far, RANKS, far)
    theirs_near = lax.ppermute(p_near, RANKS, near)

    level = lax.all_to_all(level.reshape(ring, B // ring, B), RING, 0, 0).sum(0)
    level = lax.all_to_all(copies(level, plane), PLANE, 0, 0).sum(0)
    level = level / jnp.sqrt(jnp.float32(count * B))
    level = lax.all_to_all(copies(level, ring), RING, 0, 0).reshape(B, B)

    projected = p_own + theirs_far.astype(jnp.float32) + theirs_near.astype(jnp.float32)
    return (projected.astype(jnp.bfloat16), level)


def solution(mesh):
    mesh = Mesh(mesh.devices.reshape(8, 4, 2, 4, 2), RANKS)
    return jax.shard_map(
        per_device,
        mesh=mesh,
        in_specs=(P(RANKS, None, None, None), P(), P(RANKS, None), P(RANKS, None)),
        out_specs=(P(RANKS, None), P()),
        check_vma=False,
    )
```

```python
import functools

import jax
import jax.numpy as jnp
from jax import lax
from jax.experimental import pallas as pl
from jax.experimental.pallas import tpu as pltpu
from jax.sharding import Mesh
from jax.sharding import PartitionSpec as P

LOCAL = 8
B = 128
SLOTS = 12
PAIRS = 36
RANKS = ("y", "x", "zl", "zh", "core")
RING = ("zl", "zh", "core")
PLANE = ("y", "x")


def pair_place(a, b):
    return a * (a + 1) // 2 + b


def is_odd():
    return lax.axis_index("core") == 1


def mark_kernel(count, ocol, basis, sent, sem):
    fetch = pltpu.make_async_copy(basis, sent.at[pl.ds(0, LOCAL * B), :], sem)
    fetch.start()
    first = lax.axis_index(RANKS) * LOCAL
    row = lax.broadcasted_iota(jnp.int32, (2 * LOCAL, B), 0)
    lane = lax.broadcasted_iota(jnp.int32, (2 * LOCAL, B), 1)
    marks = jnp.zeros((2 * LOCAL, B), jnp.float32)
    for r in range(LOCAL):
        mark = lane < 0
        for s in range(SLOTS):
            mark = jnp.logical_or(mark, lane == lax.rem(ocol[r, s] - first + 2 * LOCAL + count, count))
        marks = jnp.where(jnp.logical_and(mark, row == r), 1.0, marks)
    sent[LOCAL * B :, :] = marks.astype(jnp.bfloat16)
    fetch.wait()


def mark(count, ocol, basis):
    return pl.pallas_call(
        functools.partial(mark_kernel, count),
        out_shape=jax.ShapeDtypeStruct((LOCAL * B + 2 * LOCAL, B), jnp.bfloat16),
        in_specs=[pl.BlockSpec(memory_space=pltpu.SMEM), pl.BlockSpec(memory_space=pl.ANY)],
        out_specs=pl.BlockSpec(memory_space=pltpu.VMEM),
        scratch_shapes=[pltpu.SemaphoreType.DMA],
        compiler_params=pltpu.CompilerParams(vmem_limit_bytes=56 * 1024 * 1024),
        name="mark",
    )(ocol, basis)


def pack_kernel(count, tcol, tval_hbm, to_far, to_near, table, tval, sem):
    fetch = pltpu.make_async_copy(tval_hbm, tval, sem)
    fetch.start()
    odd = is_odd()
    first = lax.axis_index(RANKS) * LOCAL
    far_right = jnp.where(odd, 0, PAIRS)
    far_left = PAIRS - far_right
    for p in range(2 * PAIRS):
        table[p] = 0
    for r in range(LOCAL):
        for s in range(SLOTS):
            v = lax.rem(tcol[r, s] - first + LOCAL + count, count)
            place = jnp.where(
                v >= 2 * LOCAL,
                far_right + pair_place(r, 0) + v - 2 * LOCAL,
                jnp.where(v < LOCAL, far_left + pair_place(LOCAL - 1 - r, 0) + LOCAL - 1 - v, 2 * PAIRS),
            )
            table[place] = s
    fetch.wait()
    for a in range(LOCAL):
        far_row = jnp.where(odd, a, LOCAL - 1 - a)
        near_row = LOCAL - 1 - far_row
        for b in range(a + 1):
            p = pair_place(a, b)
            to_far[:, p * B : (p + 1) * B] = tval[far_row, table[p]]
            to_near[:, p * B : (p + 1) * B] = tval[near_row, table[PAIRS + p]]


def pack(count, tcol, tval):
    out = jax.ShapeDtypeStruct((B, PAIRS * B), jnp.bfloat16)
    vmem = pl.BlockSpec(memory_space=pltpu.VMEM)
    return pl.pallas_call(
        functools.partial(pack_kernel, count),
        out_shape=(out, out),
        in_specs=[pl.BlockSpec(memory_space=pltpu.SMEM), pl.BlockSpec(memory_space=pl.ANY)],
        out_specs=(vmem, vmem),
        scratch_shapes=[
            pltpu.SMEM((2 * PAIRS + 1,), jnp.int32),
            pltpu.VMEM((LOCAL, SLOTS, B, B), jnp.bfloat16),
            pltpu.SemaphoreType.DMA,
        ],
        compiler_params=pltpu.CompilerParams(vmem_limit_bytes=56 * 1024 * 1024),
        name="pack",
    )(tcol, tval)


def inner_kernel(tcol, wanted, held, tval, basis_far, basis, basis_near, y_out, p_out, level, basis_t, blocks, z, y_own, t_own, table):
    odd = is_odd()
    size = LOCAL * B
    far_at = jnp.where(odd, 2 * size, 0)
    blocks[pl.ds(pl.multiple_of(far_at, size), size), :] = basis_far[:size, :]
    blocks[size : 2 * size, :] = basis[...]
    blocks[pl.ds(pl.multiple_of(2 * size - far_at, size), size), :] = basis_near[:size, :]
    for p in range(LOCAL * LOCAL):
        table[p] = 0
    for r in range(LOCAL):
        for s in range(SLOTS):
            v = tcol[LOCAL + r, s] - LOCAL
            inside = jnp.logical_and(v >= 0, v < LOCAL)
            table[jnp.where(inside, r * LOCAL + v, LOCAL * LOCAL)] = s

    @pl.loop(0, LOCAL)
    def _(j):
        for s in range(SLOTS):
            c = tcol[LOCAL + j, s]
            z[s] = jnp.dot(
                tval[j, s],
                blocks[pl.ds(pl.multiple_of(c * B, B), B), :],
                preferred_element_type=jnp.float32,
            )

        @pl.loop(0, 2 * LOCAL + 1)
        def _(d):
            i = j + d
            r = i & (LOCAL - 1)
            part = i >> 3
            own = part == 1
            left = part == 0
            a = jnp.where(left, r, LOCAL - 1 - r)
            b = jnp.where(left, j, LOCAL - 1 - j)
            place = (a * (a + 1) >> 1) + b + jnp.where(left == odd, PAIRS, 0)
            place = jnp.where(own, r * LOCAL + j, place)
            rows = pl.ds(pl.multiple_of(place * B, B), B)
            on = held[i, j]

            def total():
                y = jnp.zeros((B, B), jnp.float32)
                for s in range(SLOTS):
                    y = y + wanted[i, tcol[LOCAL + j, s]] * z[s]
                return y.astype(jnp.bfloat16)

            @pl.when(jnp.logical_and(own, on == 1))
            def _():
                y_own[rows, :] = total()

            @pl.when(jnp.logical_and(jnp.logical_not(own), on == 1))
            def _():
                y_out[rows, :] = total()

            @pl.when(jnp.logical_and(own, on == 0))
            def _():
                y_own[rows, :] = jnp.zeros((B, B), jnp.bfloat16)

            @pl.when(jnp.logical_and(jnp.logical_not(own), on == 0))
            def _():
                y_out[rows, :] = jnp.zeros((B, B), jnp.bfloat16)

    level[...] = jnp.zeros((B, B), jnp.float32)

    for r in range(LOCAL):
        for j in range(LOCAL):
            t_own[r % 2, :, j * B : (j + 1) * B] = tval[r, table[r * LOCAL + j]]
        size = LOCAL * B
        p = jnp.dot(
            t_own[r % 2], y_own[r * size : (r + 1) * size, :], preferred_element_type=jnp.float32
        )
        rows = slice(r * B, (r + 1) * B)
        p_out[rows, :] = p
        level[...] += lax.dot_general(
            basis[rows, :], p.astype(jnp.bfloat16), (((0,), (0,)), ((), ())), preferred_element_type=jnp.float32
        )

    for part, ref in enumerate((basis_far, basis_near)):
        for r in range(LOCAL):
            place = (part * LOCAL + r) * B
            basis_t[:, place : place + B] = ref[r * B : (r + 1) * B, :].T


def inner(tcol, wanted, held, tval, basis_far, basis, basis_near):
    vmem = pl.BlockSpec(memory_space=pltpu.VMEM)
    smem = pl.BlockSpec(memory_space=pltpu.SMEM)
    return pl.pallas_call(
        inner_kernel,
        out_shape=(
            jax.ShapeDtypeStruct((2 * PAIRS * B, B), jnp.bfloat16),
            jax.ShapeDtypeStruct((LOCAL * B, B), jnp.float32),
            jax.ShapeDtypeStruct((B, B), jnp.float32),
            jax.ShapeDtypeStruct((B, 2 * LOCAL * B), jnp.bfloat16),
        ),
        in_specs=[smem, smem, smem, vmem, vmem, vmem, vmem],
        out_specs=(vmem, vmem, vmem, vmem),
        scratch_shapes=[
            pltpu.VMEM((3 * LOCAL * B, B), jnp.bfloat16),
            pltpu.VMEM((SLOTS, B, B), jnp.float32),
            pltpu.VMEM((LOCAL * LOCAL * B, B), jnp.bfloat16),
            pltpu.VMEM((2, B, LOCAL * B), jnp.bfloat16),
            pltpu.SMEM((LOCAL * LOCAL + 1,), jnp.int32),
        ],
        compiler_params=pltpu.CompilerParams(vmem_limit_bytes=28 * 1024 * 1024),
        cost_estimate=pl.CostEstimate(flops=12_000_000_000, bytes_accessed=8_000_000, transcendentals=0),
        name="inner",
    )(tcol, wanted, held, tval, basis_far, basis, basis_near)


def outer_kernel(side, received, y, basis_t, level_in, p_out, level):
    odd = is_odd()
    for a in range(LOCAL):
        at = pair_place(a, 0) * B
        span = (a + 1) * B
        row = jnp.where(odd == (side == 0), LOCAL - 1 - a, a)
        p = jnp.dot(received[:, at : at + span], y[at : at + span, :], preferred_element_type=jnp.float32)
        p_out[pl.ds(pl.multiple_of(row * B, B), B), :] = p.astype(jnp.bfloat16)
    level[...] = level_in[...] + jnp.dot(basis_t[...], p_out[...], preferred_element_type=jnp.float32)


def outer(side, received, y, basis_t, level, name):
    vmem = pl.BlockSpec(memory_space=pltpu.VMEM)
    rows = LOCAL * B
    return pl.pallas_call(
        functools.partial(outer_kernel, side),
        grid=(1,),
        out_shape=(jax.ShapeDtypeStruct((rows, B), jnp.bfloat16), jax.ShapeDtypeStruct((B, B), jnp.float32)),
        in_specs=[
            vmem,
            pl.BlockSpec((PAIRS * B, B), lambda i: (side, 0)),
            pl.BlockSpec((B, rows), lambda i: (0, side)),
            vmem,
        ],
        out_specs=(vmem, vmem),
        compiler_params=pltpu.CompilerParams(vmem_limit_bytes=20 * 1024 * 1024),
        cost_estimate=pl.CostEstimate(flops=400_000_000, bytes_accessed=3_000_000, transcendentals=0),
        name=name,
    )(received, y, basis_t, level)


def copies(part, count):
    return jnp.broadcast_to(part[None], (count,) + part.shape)


def per_device(tval, tcol, ocol, basis):
    devices = lax.axis_size(RANKS)
    count = LOCAL * devices
    me = lax.axis_index(RANKS)
    first = me * LOCAL
    near = [(i, i ^ 1) for i in range(devices)]
    far = [(i, (i + 1) % devices if i % 2 else (i - 1) % devices) for i in range(devices)]
    ring = lax.axis_size(RING)
    plane = lax.axis_size(PLANE)

    cols = jnp.concatenate(
        [lax.dynamic_slice_in_dim(tcol, ((me + k) % devices) * LOCAL, LOCAL, 0) for k in (devices - 1, 0, 1)]
    )
    cols = (cols - first + LOCAL + count) % count
    sent = mark(count, ocol, basis)
    basis_far = lax.ppermute(sent, RANKS, far)
    basis_near = lax.ppermute(sent, RANKS, near)
    to_far, to_near = pack(count, lax.dynamic_slice_in_dim(tcol, first, LOCAL, 0), tval)
    from_far = lax.ppermute(to_far, RANKS, far)
    from_near = lax.ppermute(to_near, RANKS, near)

    held = jnp.any(cols[:, :, None] == LOCAL + jnp.arange(LOCAL, dtype=jnp.int32), axis=1).astype(jnp.int32)
    rows = LOCAL * B
    odd = is_odd()
    far_marks, near_marks = (part[rows : rows + LOCAL] for part in (basis_far, basis_near))
    wanted = jnp.concatenate(
        [
            jnp.where(odd, near_marks, far_marks)[:, 2 * LOCAL : 5 * LOCAL],
            sent[rows : rows + LOCAL, LOCAL : 4 * LOCAL],
            jnp.where(odd, far_marks, near_marks)[:, : 3 * LOCAL],
        ]
    ).astype(jnp.float32)
    y, p_own, level, basis_t = inner(cols, wanted, held, tval, basis_far, basis, basis_near)
    p_near, level = outer(1, from_near, y, basis_t, level, "outer_near")
    p_far, level = outer(0, from_far, y, basis_t, level, "outer_far")

    theirs_far = lax.ppermute(p_far, RANKS, far)
    theirs_near = lax.ppermute(p_near, RANKS, near)

    level = lax.all_to_all(level.reshape(ring, B // ring, B), RING, 0, 0).sum(0)
    level = lax.all_to_all(copies(level.astype(jnp.bfloat16), plane), PLANE, 0, 0).astype(jnp.float32).sum(0)
    level = level / jnp.sqrt(jnp.float32(count * B))
    level = lax.all_to_all(copies(level, ring), RING, 0, 0).reshape(B, B)

    projected = p_own + theirs_far.astype(jnp.float32) + theirs_near.astype(jnp.float32)
    return (projected.astype(jnp.bfloat16), level)


def solution(mesh):
    mesh = Mesh(mesh.devices.reshape(8, 4, 2, 4, 2), RANKS)
    return jax.shard_map(
        per_device,
        mesh=mesh,
        in_specs=(P(RANKS, None, None, None), P(), P(RANKS, None), P(RANKS, None)),
        out_specs=(P(RANKS, None), P()),
        check_vma=False,
    )
```

```python
import functools

import jax
import jax.numpy as jnp
from jax import lax
from jax.experimental import pallas as pl
from jax.experimental.pallas import tpu as pltpu
from jax.sharding import Mesh
from jax.sharding import PartitionSpec as P

LOCAL = 8
B = 128
SLOTS = 12
PAIRS = 36
RANKS = ("y", "x", "zl", "zh", "core")
RING = ("zl", "zh", "core")
PLANE = ("y", "x")


def pair_place(a, b):
    return a * (a + 1) // 2 + b


def is_odd():
    return lax.axis_index("core") == 1


def mark_kernel(count, ocol, basis, sent, sem):
    fetch = pltpu.make_async_copy(basis, sent.at[pl.ds(0, LOCAL * B), :], sem)
    fetch.start()
    first = lax.axis_index(RANKS) * LOCAL
    row = lax.broadcasted_iota(jnp.int32, (2 * LOCAL, B), 0)
    lane = lax.broadcasted_iota(jnp.int32, (2 * LOCAL, B), 1)
    marks = jnp.zeros((2 * LOCAL, B), jnp.float32)
    for r in range(LOCAL):
        mark = lane < 0
        for s in range(SLOTS):
            mark = jnp.logical_or(mark, lane == lax.rem(ocol[r, s] - first + 2 * LOCAL + count, count))
        marks = jnp.where(jnp.logical_and(mark, row == r), 1.0, marks)
    sent[LOCAL * B :, :] = marks.astype(jnp.bfloat16)
    fetch.wait()


def mark(count, ocol, basis):
    return pl.pallas_call(
        functools.partial(mark_kernel, count),
        out_shape=jax.ShapeDtypeStruct((LOCAL * B + 2 * LOCAL, B), jnp.bfloat16),
        in_specs=[pl.BlockSpec(memory_space=pltpu.SMEM), pl.BlockSpec(memory_space=pl.ANY)],
        out_specs=pl.BlockSpec(memory_space=pltpu.VMEM),
        scratch_shapes=[pltpu.SemaphoreType.DMA],
        compiler_params=pltpu.CompilerParams(vmem_limit_bytes=56 * 1024 * 1024),
        name="mark",
    )(ocol, basis)


def pack_kernel(count, tcol, tval_hbm, to_far, to_near, table, tval, sem):
    fetch = pltpu.make_async_copy(tval_hbm, tval, sem)
    fetch.start()
    odd = is_odd()
    first = lax.axis_index(RANKS) * LOCAL
    far_right = jnp.where(odd, 0, PAIRS)
    far_left = PAIRS - far_right
    for p in range(2 * PAIRS):
        table[p] = 0
    for r in range(LOCAL):
        for s in range(SLOTS):
            v = lax.rem(tcol[r, s] - first + LOCAL + count, count)
            place = jnp.where(
                v >= 2 * LOCAL,
                far_right + pair_place(r, 0) + v - 2 * LOCAL,
                jnp.where(v < LOCAL, far_left + pair_place(LOCAL - 1 - r, 0) + LOCAL - 1 - v, 2 * PAIRS),
            )
            table[place] = s
    fetch.wait()
    for a in range(LOCAL):
        far_row = jnp.where(odd, a, LOCAL - 1 - a)
        near_row = LOCAL - 1 - far_row
        for b in range(a + 1):
            p = pair_place(a, b)
            to_far[:, p * B : (p + 1) * B] = tval[far_row, table[p]]
            to_near[:, p * B : (p + 1) * B] = tval[near_row, table[PAIRS + p]]


def pack(count, tcol, tval):
    out = jax.ShapeDtypeStruct((B, PAIRS * B), jnp.bfloat16)
    vmem = pl.BlockSpec(memory_space=pltpu.VMEM)
    return pl.pallas_call(
        functools.partial(pack_kernel, count),
        out_shape=(out, out),
        in_specs=[pl.BlockSpec(memory_space=pltpu.SMEM), pl.BlockSpec(memory_space=pl.ANY)],
        out_specs=(vmem, vmem),
        scratch_shapes=[
            pltpu.SMEM((2 * PAIRS + 1,), jnp.int32),
            pltpu.VMEM((LOCAL, SLOTS, B, B), jnp.bfloat16),
            pltpu.SemaphoreType.DMA,
        ],
        compiler_params=pltpu.CompilerParams(vmem_limit_bytes=56 * 1024 * 1024),
        name="pack",
    )(tcol, tval)


def inner_kernel(tcol, wanted, held, tval, basis_far, basis, basis_near, y_out, p_out, level, basis_t, blocks, z, y_own, t_own, table):
    odd = is_odd()
    size = LOCAL * B
    far_at = jnp.where(odd, 2 * size, 0)
    blocks[pl.ds(pl.multiple_of(far_at, size), size), :] = basis_far[:size, :]
    blocks[size : 2 * size, :] = basis[...]
    blocks[pl.ds(pl.multiple_of(2 * size - far_at, size), size), :] = basis_near[:size, :]
    for p in range(LOCAL * LOCAL):
        table[p] = 0
    for r in range(LOCAL):
        for s in range(SLOTS):
            v = tcol[LOCAL + r, s] - LOCAL
            inside = jnp.logical_and(v >= 0, v < LOCAL)
            table[jnp.where(inside, r * LOCAL + v, LOCAL * LOCAL)] = s

    @pl.loop(0, LOCAL)
    def _(j):
        for s in range(SLOTS):
            c = tcol[LOCAL + j, s]
            z[s] = jnp.dot(
                tval[j, s],
                blocks[pl.ds(pl.multiple_of(c * B, B), B), :],
                preferred_element_type=jnp.float32,
            )

        @pl.loop(0, 2 * LOCAL + 1)
        def _(d):
            i = j + d
            r = i & (LOCAL - 1)
            part = i >> 3
            own = part == 1
            left = part == 0
            a = jnp.where(left, r, LOCAL - 1 - r)
            b = jnp.where(left, j, LOCAL - 1 - j)
            place = (a * (a + 1) >> 1) + b + jnp.where(left == odd, PAIRS, 0)
            place = jnp.where(own, r * LOCAL + j, place)
            rows = pl.ds(pl.multiple_of(place * B, B), B)
            on = held[i, j]

            def total():
                y = jnp.zeros((B, B), jnp.float32)
                for s in range(SLOTS):
                    y = y + wanted[i, tcol[LOCAL + j, s]] * z[s]
                return y.astype(jnp.bfloat16)

            @pl.when(jnp.logical_and(own, on == 1))
            def _():
                y_own[rows, :] = total()

            @pl.when(jnp.logical_and(jnp.logical_not(own), on == 1))
            def _():
                y_out[rows, :] = total()

            @pl.when(jnp.logical_and(own, on == 0))
            def _():
                y_own[rows, :] = jnp.zeros((B, B), jnp.bfloat16)

            @pl.when(jnp.logical_and(jnp.logical_not(own), on == 0))
            def _():
                y_out[rows, :] = jnp.zeros((B, B), jnp.bfloat16)

    level[...] = jnp.zeros((B, B), jnp.float32)

    for r in range(LOCAL):
        for j in range(LOCAL):
            t_own[r % 2, :, j * B : (j + 1) * B] = tval[r, table[r * LOCAL + j]]
        size = LOCAL * B
        p = jnp.dot(
            t_own[r % 2], y_own[r * size : (r + 1) * size, :], preferred_element_type=jnp.float32
        )
        rows = slice(r * B, (r + 1) * B)
        p_out[rows, :] = p
        level[...] += lax.dot_general(
            basis[rows, :], p.astype(jnp.bfloat16), (((0,), (0,)), ((), ())), preferred_element_type=jnp.float32
        )

    for part, ref in enumerate((basis_far, basis_near)):
        for r in range(LOCAL):
            place = (part * LOCAL + r) * B
            basis_t[:, place : place + B] = ref[r * B : (r + 1) * B, :].T


def inner(tcol, wanted, held, tval, basis_far, basis, basis_near):
    vmem = pl.BlockSpec(memory_space=pltpu.VMEM)
    smem = pl.BlockSpec(memory_space=pltpu.SMEM)
    return pl.pallas_call(
        inner_kernel,
        out_shape=(
            jax.ShapeDtypeStruct((2 * PAIRS * B, B), jnp.bfloat16),
            jax.ShapeDtypeStruct((LOCAL * B, B), jnp.float32),
            jax.ShapeDtypeStruct((B, B), jnp.float32),
            jax.ShapeDtypeStruct((B, 2 * LOCAL * B), jnp.bfloat16),
        ),
        in_specs=[smem, smem, smem, vmem, vmem, vmem, vmem],
        out_specs=(vmem, vmem, vmem, vmem),
        scratch_shapes=[
            pltpu.VMEM((3 * LOCAL * B, B), jnp.bfloat16),
            pltpu.VMEM((SLOTS, B, B), jnp.float32),
            pltpu.VMEM((LOCAL * LOCAL * B, B), jnp.bfloat16),
            pltpu.VMEM((2, B, LOCAL * B), jnp.bfloat16),
            pltpu.SMEM((LOCAL * LOCAL + 1,), jnp.int32),
        ],
        compiler_params=pltpu.CompilerParams(vmem_limit_bytes=28 * 1024 * 1024),
        cost_estimate=pl.CostEstimate(flops=12_000_000_000, bytes_accessed=8_000_000, transcendentals=0),
        name="inner",
    )(tcol, wanted, held, tval, basis_far, basis, basis_near)


def outer_kernel(side, received, y, basis_t, level_in, earlier, p_out, level):
    del earlier
    odd = is_odd()
    for a in range(LOCAL):
        at = pair_place(a, 0) * B
        span = (a + 1) * B
        row = jnp.where(odd == (side == 0), LOCAL - 1 - a, a)
        p = jnp.dot(received[:, at : at + span], y[at : at + span, :], preferred_element_type=jnp.float32)
        p_out[pl.ds(pl.multiple_of(row * B, B), B), :] = p.astype(jnp.bfloat16)
    level[...] = level_in[...] + jnp.dot(basis_t[...], p_out[...], preferred_element_type=jnp.float32)


def outer(side, received, y, basis_t, level, earlier, name):
    vmem = pl.BlockSpec(memory_space=pltpu.VMEM)
    rows = LOCAL * B
    return pl.pallas_call(
        functools.partial(outer_kernel, side),
        grid=(1,),
        out_shape=(jax.ShapeDtypeStruct((rows, B), jnp.bfloat16), jax.ShapeDtypeStruct((B, B), jnp.float32)),
        in_specs=[
            vmem,
            pl.BlockSpec((PAIRS * B, B), lambda i: (side, 0)),
            pl.BlockSpec((B, rows), lambda i: (0, side)),
            vmem,
            pl.BlockSpec(memory_space=pl.ANY),
        ],
        out_specs=(vmem, vmem),
        compiler_params=pltpu.CompilerParams(vmem_limit_bytes=20 * 1024 * 1024),
        cost_estimate=pl.CostEstimate(flops=400_000_000, bytes_accessed=3_000_000, transcendentals=0),
        name=name,
    )(received, y, basis_t, level, earlier)


def copies(part, count):
    return jnp.broadcast_to(part[None], (count,) + part.shape)


def per_device(tval, tcol, ocol, basis):
    devices = lax.axis_size(RANKS)
    count = LOCAL * devices
    me = lax.axis_index(RANKS)
    first = me * LOCAL
    near = [(i, i ^ 1) for i in range(devices)]
    far = [(i, (i + 1) % devices if i % 2 else (i - 1) % devices) for i in range(devices)]
    ring = lax.axis_size(RING)
    plane = lax.axis_size(PLANE)

    cols = jnp.concatenate(
        [lax.dynamic_slice_in_dim(tcol, ((me + k) % devices) * LOCAL, LOCAL, 0) for k in (devices - 1, 0, 1)]
    )
    cols = (cols - first + LOCAL + count) % count
    sent = mark(count, ocol, basis)
    basis_far = lax.ppermute(sent, RANKS, far)
    basis_near = lax.ppermute(sent, RANKS, near)
    to_far, to_near = pack(count, lax.dynamic_slice_in_dim(tcol, first, LOCAL, 0), tval)
    from_far = lax.ppermute(to_far, RANKS, far)
    from_near = lax.ppermute(to_near, RANKS, near)

    held = jnp.any(cols[:, :, None] == LOCAL + jnp.arange(LOCAL, dtype=jnp.int32), axis=1).astype(jnp.int32)
    rows = LOCAL * B
    odd = is_odd()
    far_marks, near_marks = (part[rows : rows + LOCAL] for part in (basis_far, basis_near))
    wanted = jnp.concatenate(
        [
            jnp.where(odd, near_marks, far_marks)[:, 2 * LOCAL : 5 * LOCAL],
            sent[rows : rows + LOCAL, LOCAL : 4 * LOCAL],
            jnp.where(odd, far_marks, near_marks)[:, : 3 * LOCAL],
        ]
    ).astype(jnp.float32)
    y, p_own, level, basis_t = inner(cols, wanted, held, tval, basis_far, basis, basis_near)
    p_near, level = outer(1, from_near, y, basis_t, level, level, "outer_near")
    theirs_near = lax.ppermute(p_near, RANKS, near)
    p_far, level = outer(0, from_far, y, basis_t, level, theirs_near, "outer_far")

    theirs_far = lax.ppermute(p_far, RANKS, far)

    level = lax.all_to_all(level.reshape(ring, B // ring, B), RING, 0, 0).sum(0)
    level = lax.all_to_all(copies(level.astype(jnp.bfloat16), plane), PLANE, 0, 0).astype(jnp.float32).sum(0)
    level = level / jnp.sqrt(jnp.float32(count * B))
    level = lax.all_to_all(copies(level, ring), RING, 0, 0).reshape(B, B)

    projected = p_own + theirs_far.astype(jnp.float32) + theirs_near.astype(jnp.float32)
    return (projected.astype(jnp.bfloat16), level)


def solution(mesh):
    mesh = Mesh(mesh.devices.reshape(8, 4, 2, 4, 2), RANKS)
    return jax.shard_map(
        per_device,
        mesh=mesh,
        in_specs=(P(RANKS, None, None, None), P(), P(RANKS, None), P(RANKS, None)),
        out_specs=(P(RANKS, None), P()),
        check_vma=False,
    )
```
